32 devices in a mesh: img: 4 (over x, core), txt: 8 (over z, y).
Axes of the slice: x: 2, y: 2, z: 4, core: 2. Of those that a mesh axis runs over, the one named last changes fastest.
Arguments:
- images: bfloat16 [1536, 1152], P(('img', 'txt')), may hold values from -36 to 36
- texts: bfloat16 [1536, 640], P(('txt', 'img')), may hold values from -36 to 36
- head_weight: bfloat16 [1152, 640], replicated, may hold values from -0.088388348 to 0.088388348
- log_scale: float32 [1], replicated, may hold values from 1.5 to 2.5
- logit_bias: float32 [1], replicated, may hold values from -4 to -1
Outputs:
- image_grads: bfloat16 [1536, 1152], P(('img', 'txt'))
- text_grads: bfloat16 [1536, 640], P(('txt', 'img'))
- head_grad: float32 [1152, 640], replicated
The draws below stay inside these ranges and needn't reach their ends.
All inputs are finite; a program needn't handle non-finite values.
Results may differ from the reference program's by a relative error of at most 0.02.
Values may be sent and summed in bfloat16 or wider, within the bound.
No kernel may reach another device: no remote copies, remote signals or barrier semaphores. Data moves between devices by JAX's collectives and lax.ppermute only.
A program may use at most 64 MiB of HBM per device.

```python
import math
import jax
import jax.numpy as jnp
from jax import lax

EMB = 1152
PROJ = 640
PAIRS = 1536
IMG_ROWS = 384
TXT_ROWS = 192
N_IMG = 4
N_TXT = 8


def shared_layout(key):
    key_weight, key_member, key_start, key_sign = jax.random.split(key, 4)
    weight = jnp.clip(jax.random.normal(key_weight, (EMB, PROJ), jnp.float32), -3.0, 3.0) * EMB ** (-0.5)
    groups = max(PAIRS // 64, 2)
    member_ids = jax.random.randint(key_member, (PAIRS,), 0, groups)
    start_rows = jax.random.randint(key_start, (groups, 1), 0, EMB)
    picked_rows = (start_rows + jnp.arange(4, dtype=jnp.int32)[None, :] * (EMB // 4)) % EMB
    sign_table = (2 * jax.random.randint(key_sign, (groups, 4), 0, 2) - 1).astype(jnp.float32)
    return (weight, member_ids, picked_rows, sign_table)


def noise_field(key, rows, cols):
    key_rows, key_cols, key_base = jax.random.split(key, 3)
    row_scale = jnp.exp(jax.random.uniform(key_rows, (rows, 1), jnp.float32, math.log(0.3), math.log(3.0)))
    col_scale = jnp.exp(jax.random.uniform(key_cols, (1, cols), jnp.float32, math.log(0.3), math.log(3.0)))
    base = 0.5 * jnp.clip(jax.random.normal(key_base, (rows, cols), jnp.float32), -2.0, 2.0)
    return (base * col_scale, row_scale)


def draw_head_weight(key, part):
    weight, member_ids, picked_rows, sign_table = shared_layout(key)
    return weight.astype(jnp.bfloat16)


def draw_images(key, part):
    weight, member_ids, picked_rows, sign_table = shared_layout(key)
    key = jax.random.fold_in(key, 11)
    positions = jnp.arange(EMB, dtype=jnp.int32)[None, :]
    spikes = jnp.where(positions == picked_rows[:, 0:1], sign_table[:, 0:1], 0.0)
    spikes = spikes + jnp.where(positions == picked_rows[:, 1:2], sign_table[:, 1:2], 0.0)
    spikes = spikes + jnp.where(positions == picked_rows[:, 2:3], sign_table[:, 2:3], 0.0)
    spikes = spikes + jnp.where(positions == picked_rows[:, 3:4], sign_table[:, 3:4], 0.0)
    noise, row_scale = noise_field(key, PAIRS, EMB)
    field = row_scale * (9.0 * spikes[member_ids] + noise)
    return jnp.clip(field, -36.0, 36.0).astype(jnp.bfloat16)


def draw_texts(key, part):
    weight, member_ids, picked_rows, sign_table = shared_layout(key)
    key = jax.random.fold_in(key, 23)
    first = sign_table[:, 0:1] * weight[picked_rows[:, 0]]
    second = sign_table[:, 1:2] * weight[picked_rows[:, 1]]
    third = sign_table[:, 2:3] * weight[picked_rows[:, 2]]
    fourth = sign_table[:, 3:4] * weight[picked_rows[:, 3]]
    centres = (first + second + third + fourth) * (0.5 * EMB ** 0.5)
    noise, row_scale = noise_field(key, PAIRS, PROJ)
    field = row_scale * (1.2 * centres[member_ids] + noise)
    return jnp.clip(field, -36.0, 36.0).astype(jnp.bfloat16)


def setup_inputs(seed: int = 0) -> dict:
    seeds = jax.random.split(jax.random.key(seed), 6)
    return {
        "images": draw_images(jax.random.fold_in(seeds[5], 71), 0),
        "texts": draw_texts(jax.random.fold_in(seeds[5], 71), 0),
        "head_weight": draw_head_weight(jax.random.fold_in(seeds[5], 71), 0),
        "log_scale": jnp.clip(jax.random.uniform(seeds[3], (1,), jnp.float32, 1.5, 2.5), 1.5, 2.5),
        "logit_bias": jnp.clip(jax.random.uniform(seeds[4], (1,), jnp.float32, -4.0, -1.0), -4.0, -1.0),
    }


eps = 1e-06

def reference(images, texts, head_weight, log_scale, logit_bias):
    scale = jnp.exp(log_scale[0])
    bias = logit_bias[0]
    hidden = jnp.dot(images, head_weight, preferred_element_type=jnp.float32)
    img_inv = lax.rsqrt(lax.optimization_barrier(jnp.sum(hidden * hidden, axis=1, keepdims=True)) + eps)
    img_unit = (hidden * img_inv).astype(jnp.bfloat16)
    txt_full = texts.astype(jnp.float32)
    txt_inv = lax.rsqrt(lax.optimization_barrier(jnp.sum(txt_full * txt_full, axis=1, keepdims=True)) + eps)
    txt_unit = (txt_full * txt_inv).astype(jnp.bfloat16)
    total = img_unit.shape[0]
    features = img_unit.shape[1]
    blocks = img_unit.reshape(N_IMG, IMG_ROWS, features)
    txt_groups = txt_unit.astype(jnp.float32).reshape(N_TXT, TXT_ROWS, features)
    columns = jnp.arange(total, dtype=jnp.int32)

    def step(carry, inputs):
        block, index = inputs
        logits = scale * jnp.dot(block, txt_unit.T, preferred_element_type=jnp.float32) + bias
        row_ids = index * IMG_ROWS + jnp.arange(IMG_ROWS, dtype=jnp.int32)
        label = jnp.where(row_ids[:, None] == columns[None, :], 1.0, -1.0).astype(jnp.float32)
        grad = (-label * jax.nn.sigmoid(-label * logits)).astype(jnp.bfloat16)
        grad_groups = grad.astype(jnp.float32).reshape(IMG_ROWS, N_TXT, TXT_ROWS)
        partials = scale * jnp.einsum('rgc,gcf->grf', grad_groups, txt_groups)
        partials = partials.astype(jnp.bfloat16).astype(jnp.float32)
        d_rows = lax.optimization_barrier(jnp.sum(partials, axis=0))
        txt_part = scale * lax.dot_general(grad, block, (((0,), (0,)), ((), ())), preferred_element_type=jnp.float32)
        carry = carry + txt_part.astype(jnp.bfloat16).astype(jnp.float32)
        return (carry, d_rows)
    d_txt, d_parts = lax.scan(step, jnp.zeros(txt_unit.shape, jnp.float32), (blocks, jnp.arange(N_IMG, dtype=jnp.int32)))
    d_img = d_parts.reshape(total, features)
    inner = lax.optimization_barrier(jnp.sum(hidden * d_img, axis=1, keepdims=True))
    d_hidden = (img_inv * (d_img - hidden * img_inv * img_inv * inner)).astype(jnp.bfloat16)
    image_grads = jnp.dot(d_hidden, head_weight.T, preferred_element_type=jnp.float32).astype(jnp.bfloat16)
    head_grad = lax.dot_general(images, d_hidden, (((0,), (0,)), ((), ())), preferred_element_type=jnp.float32)
    inner_txt = lax.optimization_barrier(jnp.sum(txt_full * d_txt, axis=1, keepdims=True))
    text_grads = (txt_inv * (d_txt - txt_full * txt_inv * txt_inv * inner_txt)).astype(jnp.bfloat16)
    return (image_grads, text_grads, head_grad)
```

```python
import functools

import jax
import jax.numpy as jnp
import numpy as np
from jax import lax
from jax.experimental import pallas as pl
from jax.experimental.pallas import tpu as pltpu
from jax.sharding import PartitionSpec as P

eps = 1e-06
f32, bf16 = jnp.float32, jnp.bfloat16
NT = (((1,), (1,)), ((), ()))
TN = (((0,), (0,)), ((), ()))
VMEM = pl.BlockSpec(memory_space=pltpu.VMEM)
SMEM = pl.BlockSpec(memory_space=pltpu.SMEM)
LIMIT = 32 * 1024 * 1024
GATHER_BYTES = 8 * 1024 * 1024


def dot(a, b, dims=(((1,), (0,)), ((), ()))):
    return lax.dot_general(a, b, dims, preferred_element_type=f32)


def call(body, out_shape, in_specs, flops, scratch=()):
    return pl.pallas_call(
        body,
        out_shape=out_shape,
        in_specs=in_specs,
        out_specs=jax.tree.map(lambda _: VMEM, out_shape),
        scratch_shapes=scratch,
        compiler_params=pltpu.CompilerParams(vmem_limit_bytes=LIMIT),
        cost_estimate=pl.CostEstimate(flops=flops, bytes_accessed=4_000_000, transcendentals=0),
    )


def unit_body(*refs):
    out = refs[-1]
    first = 0
    for ref in refs[:-1]:
        rows = ref.shape[0]
        full = ref[...].astype(f32)
        inv = lax.rsqrt(jnp.sum(full * full, axis=1, keepdims=True) + eps)
        out[pl.ds(first, rows), :] = (full * inv).astype(bf16)
        first += rows


def chunks(total):
    width = 256
    return [(c, min(width, total - c)) for c in range(0, total, width)]


def batch_body(first, scalars, img_a, img_b, weight, txt_own, txt_sib, row_ids, col_ids, *refs):
    if first:
        d_hidden_ref, own_ref, sib_ref, grads_ref, hidden_ref, unit_ref, d_img_ref = refs
    else:
        own_in, sib_in, d_hidden_ref, own_ref, sib_ref, hidden_ref, unit_ref, d_img_ref = refs
    scale, bias = scalars[0], scalars[1]
    half = img_a.shape[0]
    rows = 2 * half
    block = own_ref.shape[0]
    for at, ref in ((0, img_a), (half, img_b)):
        hidden_ref[pl.ds(at, half), :] = dot(ref[...], weight[...])
    hidden = hidden_ref[...]
    inv = lax.rsqrt(jnp.sum(hidden * hidden, axis=1, keepdims=True) + eps)
    unit_ref[...] = (hidden * inv).astype(bf16)
    ids = row_ids[...]
    begun = False
    for side, txt in enumerate((txt_own, txt_sib)):
        total = txt.shape[0]
        for at, width in chunks(total):
            text = txt[pl.ds(at, width), :]
            logits = scale * dot(unit_ref[...], text, NT) + bias
            same = ids == col_ids[:, pl.ds(side * total + at, width)]
            flip = jnp.where(same, -1.0, 1.0)
            grad = (flip * jax.nn.sigmoid(flip * logits)).astype(bf16)
            part = dot(grad, text)
            d_img_ref[...] = d_img_ref[...] + part if begun else part
            begun = True
            if at == 0:
                edge = min(128, width)
                term = dot(grad[:, :edge], unit_ref[...], TN)[:block, :]
                ref = (own_ref, sib_ref)[side]
                ref[...] = term if first else term + (own_in, sib_in)[side][...]
    d_img = scale * d_img_ref[...]
    hidden = hidden_ref[...]
    inner = jnp.sum(hidden * d_img, axis=1, keepdims=True)
    d_hidden = (inv * (d_img - hidden * (inv * inv * inner))).astype(bf16)
    d_hidden_ref[...] = d_hidden
    if first:
        grads_ref[...] = dot(d_hidden[:block, :], weight[...], NT).astype(bf16)


def head_body(count, *refs):
    images, d_hidden, out = refs[:count], refs[count:-1], refs[-1]
    left = jnp.concatenate([ref[...] for ref in images], axis=0)
    right = jnp.concatenate([ref[...] for ref in d_hidden], axis=0)
    out[...] = dot(left, right, TN)


def text_body(scalars, texts, own, received, out):
    full = texts[...].astype(f32)
    inv = lax.rsqrt(jnp.sum(full * full, axis=1, keepdims=True) + eps)
    d_txt = scalars[0] * (own[...] + received[...])
    inner = jnp.sum(full * d_txt, axis=1, keepdims=True)
    out[...] = (inv * (d_txt - full * (inv * inv * inner))).astype(bf16)


def gathered(n_img, n_txt, images, texts, head_weight, log_scale, logit_bias):
    rows, emb = images.shape
    features = texts.shape[1]

    def move(array, axis, mask):
        size = n_img if axis == "img" else n_txt
        return lax.ppermute(array, axis, [(i, i ^ mask) for i in range(size)])

    core = functools.partial(move, axis="img", mask=1)
    over_x = functools.partial(move, axis="img", mask=2)
    over_y = functools.partial(move, axis="txt", mask=1)

    def over_z(block):
        return [block] + [move(block, "txt", mask) for mask in range(2, n_txt, 2)]

    def stack(*blocks):
        return jnp.concatenate(blocks, axis=0)

    def spread(blocks):
        middle = len(blocks) // 2
        a, b = stack(*blocks[:middle]), stack(*blocks[middle:])
        a, b = stack(a, over_y(a)), stack(b, over_x(b))
        return a, b, over_x(a), over_y(b)

    z = list(range(0, n_txt, 2))
    middle = len(z) // 2
    a = [(m, 0) for m in z[:middle]] + [(m ^ 1, 0) for m in z[:middle]]
    b = [(m, 0) for m in z[middle:]] + [(m, 2) for m in z[middle:]]
    order = a + b + [(t, i ^ 2) for t, i in a] + [(t ^ 1, i) for t, i in b]
    txt_at, img_at = lax.axis_index("txt"), lax.axis_index("img")
    within = np.tile(np.arange(rows, dtype=np.int32), len(order))
    txt_mask = np.repeat(np.array([t for t, _ in order], np.int32), rows)
    img_mask = np.repeat(np.array([i for _, i in order], np.int32), rows)
    row_ids = ((img_at ^ img_mask) * n_txt + (txt_at ^ txt_mask)) * rows + within
    own_ids = ((txt_at ^ txt_mask) * n_img + (img_at ^ img_mask)) * rows + within
    sib_ids = ((txt_at ^ txt_mask) * n_img + (img_at ^ 1 ^ img_mask)) * rows + within
    col_ids = stack(own_ids, sib_ids)[None, :]
    row_ids = row_ids[:, None]

    scalars = jnp.concatenate([jnp.exp(log_scale), logit_bias])
    txt_z = over_z(texts)
    images_later, _ = lax.optimization_barrier((images, txt_z[1]))
    img_z = over_z(images_later)
    txt_parts = spread(txt_z)
    total = len(order) * rows
    txt_own = call(unit_body, jax.ShapeDtypeStruct((total, features), bf16), [VMEM] * 4, 0)(*txt_parts)
    txt_sib = core(txt_own)
    img_parts = spread(img_z)
    sib_parts = [core(part) for part in img_parts]

    batch = total // 2
    term = jax.ShapeDtypeStruct((rows, features), f32)
    d_shape = jax.ShapeDtypeStruct((batch, features), bf16)
    scratch = [
        pltpu.VMEM((batch, features), f32),
        pltpu.VMEM((batch, features), bf16),
        pltpu.VMEM((batch, features), f32),
    ]
    flops = 2 * batch * features * (emb + 4 * total)
    d_first, own, sib, image_grads = call(
        functools.partial(batch_body, True),
        (d_shape, term, term, jax.ShapeDtypeStruct((rows, emb), bf16)),
        [SMEM] + [VMEM] * 7,
        flops,
        scratch,
    )(scalars, *img_parts[:2], head_weight, txt_own, txt_sib, row_ids[:batch], col_ids)
    d_first_sib = core(d_first)
    d_second, own, sib = call(
        functools.partial(batch_body, False),
        (d_shape, term, term),
        [SMEM] + [VMEM] * 9,
        flops,
        scratch,
    )(scalars, *img_parts[2:], head_weight, txt_own, txt_sib, row_ids[batch:], col_ids, own, sib)
    d_second_sib = core(d_second)
    received = core(sib)
    text_grads = call(
        text_body, jax.ShapeDtypeStruct((rows, features), bf16), [SMEM] + [VMEM] * 3, 0
    )(scalars, texts, own, received)

    pieces = list(img_parts) + sib_parts
    d_all = [d_first, d_second, d_first_sib, d_second_sib]
    wide = 3 if emb % 384 == 0 else 1
    head_grad = pl.pallas_call(
        functools.partial(head_body, len(pieces)),
        grid=(wide,),
        out_shape=jax.ShapeDtypeStruct((emb, features), f32),
        in_specs=[pl.BlockSpec((p.shape[0], emb // wide), lambda i: (0, i)) for p in pieces]
        + [pl.BlockSpec(d.shape, lambda i: (0, 0)) for d in d_all],
        out_specs=pl.BlockSpec((emb // wide, features), lambda i: (i, 0)),
        compiler_params=pltpu.CompilerParams(vmem_limit_bytes=LIMIT),
        cost_estimate=pl.CostEstimate(
            flops=4 * total * emb * features, bytes_accessed=8_000_000, transcendentals=0
        ),
    )(*pieces, *d_all)
    return image_grads, text_grads, head_grad


def blocked(images, texts, head_weight, log_scale, logit_bias):
    scale = jnp.exp(log_scale[0])
    bias = logit_bias[0]
    hidden = jnp.dot(images, head_weight, preferred_element_type=f32)
    img_inv = lax.rsqrt(jnp.sum(hidden * hidden, axis=1, keepdims=True) + eps)
    img_unit = (hidden * img_inv).astype(bf16)
    txt_full = texts.astype(f32)
    txt_inv = lax.rsqrt(jnp.sum(txt_full * txt_full, axis=1, keepdims=True) + eps)
    txt_unit = (txt_full * txt_inv).astype(bf16)
    img_block = lax.all_gather(img_unit, "txt", axis=0, tiled=True)
    txt_block = lax.all_gather(txt_unit, "img", axis=0, tiled=True)
    total_rows = img_block.shape[0]
    total_cols = txt_block.shape[0]
    features = img_block.shape[1]
    row_first = lax.axis_index("img") * total_rows
    col_first = lax.axis_index("txt") * total_cols
    columns = col_first + jnp.arange(total_cols, dtype=jnp.int32)
    width = 512 if total_rows % 512 == 0 else total_rows
    count = total_rows // width
    blocks = img_block.reshape(count, width, features)

    def step(carry, inputs):
        block, index = inputs
        logits = scale * dot(block, txt_block, NT) + bias
        row_ids = row_first + index * width + jnp.arange(width, dtype=jnp.int32)
        label = jnp.where(row_ids[:, None] == columns[None, :], 1.0, -1.0).astype(f32)
        grad = (-label * jax.nn.sigmoid(-label * logits)).astype(bf16)
        d_rows = scale * dot(grad, txt_block)
        carry = carry + scale * dot(grad, block, TN)
        return (carry, d_rows)

    txt_terms, row_terms = lax.scan(
        step,
        jnp.zeros((total_cols, features), f32),
        (blocks, jnp.arange(count, dtype=jnp.int32)),
    )
    img_terms = row_terms.reshape(total_rows, features)
    d_img = lax.psum_scatter(
        img_terms.astype(bf16), "txt", scatter_dimension=0, tiled=True
    ).astype(f32)
    inner = jnp.sum(hidden * d_img, axis=1, keepdims=True)
    d_hidden = (img_inv * (d_img - hidden * img_inv * img_inv * inner)).astype(bf16)
    image_grads = dot(d_hidden, head_weight, NT).astype(bf16)
    head_grad = lax.psum(dot(images, d_hidden, TN), ("img", "txt"))
    d_txt = lax.psum_scatter(
        txt_terms.astype(bf16), "img", scatter_dimension=0, tiled=True
    ).astype(f32)
    inner_txt = jnp.sum(txt_full * d_txt, axis=1, keepdims=True)
    text_grads = (txt_inv * (d_txt - txt_full * txt_inv * txt_inv * inner_txt)).astype(bf16)
    return (image_grads, text_grads, head_grad)


def solution(mesh):
    n_img, n_txt = mesh.shape["img"], mesh.shape["txt"]

    def shards(images, texts, head_weight, log_scale, logit_bias):
        width = images.shape[1] + texts.shape[1]
        held = 2 * n_img * n_txt * images.shape[0] * width
        same = images.shape[0] == texts.shape[0]
        if n_img == 4 and n_txt % 4 == 0 and same and held <= GATHER_BYTES:
            return gathered(n_img, n_txt, images, texts, head_weight, log_scale, logit_bias)
        return blocked(images, texts, head_weight, log_scale, logit_bias)

    return jax.shard_map(
        shards,
        mesh=mesh,
        in_specs=(P(("img", "txt"), None), P(("txt", "img"), None), P(), P(), P()),
        out_specs=(P(("img", "txt"), None), P(("txt", "img"), None), P()),
        check_vma=False,
    )
```

```python
import functools

import jax
import jax.numpy as jnp
import numpy as np
from jax import lax
from jax.experimental import pallas as pl
from jax.experimental.pallas import tpu as pltpu
from jax.sharding import PartitionSpec as P

eps = 1e-06
f32, bf16 = jnp.float32, jnp.bfloat16
NT = (((1,), (1,)), ((), ()))
TN = (((0,), (0,)), ((), ()))
VMEM = pl.BlockSpec(memory_space=pltpu.VMEM)
ANY = pl.BlockSpec(memory_space=pl.ANY)
SMEM = pl.BlockSpec(memory_space=pltpu.SMEM)
LIMIT = 32 * 1024 * 1024
GATHER_BYTES = 8 * 1024 * 1024


def dot(a, b, dims=(((1,), (0,)), ((), ()))):
    return lax.dot_general(a, b, dims, preferred_element_type=f32)


def call(body, out_shape, in_specs, flops, scratch=()):
    return pl.pallas_call(
        body,
        out_shape=out_shape,
        in_specs=in_specs,
        out_specs=jax.tree.map(lambda _: VMEM, out_shape),
        scratch_shapes=scratch,
        compiler_params=pltpu.CompilerParams(vmem_limit_bytes=LIMIT),
        cost_estimate=pl.CostEstimate(flops=flops, bytes_accessed=0, transcendentals=0),
    )


def source(place, side, entry):
    z, first, second = entry
    over = (place[2], place[3]) if side == 0 else (place[3], place[2])
    mask = first * over[0] + second * over[1]
    return place[0] ^ (2 * (mask // 2)), place[1] ^ z ^ lax.rem(mask, 2)


def unit_body(order, n_img, place, half, other, *outs):
    outs, whole, ids = outs[:-2], outs[-2], outs[-1]
    rows = half.shape[0]
    block = 2 * rows // len(order)
    total = 2 * rows
    lane = lax.broadcasted_iota(jnp.int32, ids.shape, 1)
    found = jnp.zeros(ids.shape, jnp.int32)
    for k, entry in enumerate(order):
        for side in (0, 1):
            img, txt = source(place, side, entry)
            first_id = (txt * n_img + (img ^ side)) * block
            at = side * total + k * block
            here = jnp.logical_and(lane >= at, lane < at + block)
            found = jnp.where(here, first_id - at + lane, found)
    ids[...] = found
    step = 16 * (rows // 48)
    while rows % step or outs[0].shape[0] % step:
        step -= 16
    for at in range(0, total, step):
        ref = half if at < rows else other
        full = ref[pl.ds(at % rows, step), :].astype(f32)
        inv = lax.rsqrt(jnp.sum(full * full, axis=1, keepdims=True) + eps)
        size = outs[0].shape[0]
        unit = (full * inv).astype(bf16)
        whole[pl.ds(at, step), :] = unit
        outs[at // size][pl.ds(at % size, step), :] = unit


def batch_body(first, order, n_txt, place, scale_ref, bias_ref, images, weight, txt_own, txt_sib, col_ids, *refs):
    if first:
        d_hidden_ref, own_ref, sib_ref, hidden_ref, unit_ref, grad_ref = refs
    else:
        own_in, sib_in, d_hidden_ref, own_ref, sib_ref, hidden_ref, unit_ref, grad_ref = refs
    scale, bias = scale_ref[0:1, 0:1], bias_ref[0:1, 0:1]
    block = own_ref.shape[0]
    hidden = dot(images[...], weight[...])
    inv = lax.rsqrt(jnp.sum(hidden * hidden, axis=1, keepdims=True) + eps)
    hidden_ref[...] = hidden
    unit_ref[...] = (hidden * inv).astype(bf16)
    ids = []
    for entry in order:
        img, txt = source(place, 0, entry)
        within = lax.broadcasted_iota(jnp.int32, (block, 1), 0)
        ids.append((img * n_txt + txt) * block + within)
    ids = jnp.concatenate(ids, axis=0)
    total = txt_own.shape[0]
    width = 256 if total % 256 == 0 else total
    for side, txt in enumerate((txt_own, txt_sib)):
        for at in range(0, total, width):
            columns = pl.ds(side * total + at, width)
            logits = scale * dot(unit_ref[...], txt[pl.ds(at, width), :], NT) + bias
            flip = jnp.where(ids == col_ids[:, columns], -1.0, 1.0)
            grad_ref[:, columns] = (flip * jax.nn.sigmoid(flip * logits)).astype(bf16)
    edge = 64
    both = jnp.concatenate([grad_ref[:, pl.ds(at, edge)] for at in (0, total)], axis=1)
    terms = dot(both, unit_ref[...], TN)
    for at, ref in ((0, own_ref), (edge, sib_ref)):
        ref[...] = terms[at : at + block, :]
    if not first:
        own_ref[...] += own_in[...]
        sib_ref[...] += sib_in[...]
    d_img = dot(grad_ref[:, pl.ds(0, total)], txt_own[...])
    d_img = scale * (d_img + dot(grad_ref[:, pl.ds(total, total)], txt_sib[...]))
    hidden = hidden_ref[...]
    inner = jnp.sum(hidden * d_img, axis=1, keepdims=True)
    d_hidden_ref[...] = (inv * (d_img - hidden * (inv * inv * inner))).astype(bf16)


def begin_body(log_scale, logit_bias, texts, images, _, texts_out, images_out, scale, bias):
    scale[...] = jnp.exp(jnp.full(scale.shape, log_scale[0], f32))
    bias[...] = jnp.full(bias.shape, logit_bias[0], f32)
    texts_out[...] = texts[...]
    images_out[...] = images[...]


def join_body(*refs):
    out, at = refs[-1], 0
    for ref in refs[:-1]:
        out[pl.ds(at, ref.shape[0]), :] = ref[...]
        at += ref.shape[0]


def head_early_body(count, weight, *refs):
    images, d_hidden, (out, grads) = refs[:count], refs[count:-2], refs[-2:]
    left = jnp.concatenate([ref[...] for ref in images], axis=0)
    right = jnp.concatenate([ref[...] for ref in d_hidden], axis=0)
    out[...] = dot(left, right, TN)
    mine = d_hidden[0][pl.ds(0, grads.shape[0]), :]
    grads[...] = dot(weight[...], mine, NT).T.astype(bf16)


def last_body(count, d_count, sizes, scale, texts, own, received, *refs):
    images, d_hidden = refs[:count], refs[count : count + d_count]
    before, out, text_out, held, text_held, sems = refs[count + d_count :]
    right = jnp.concatenate([ref[...] for ref in d_hidden], axis=0)
    copies = []
    first = 0
    for k, size in enumerate(sizes):
        at = pl.ds(first, size)
        first += size
        left = jnp.concatenate([ref[:, at] for ref in images], axis=0)
        held[at, :] = before[at, :] + dot(left, right, TN)
        copies.append(pltpu.make_async_copy(held.at[at, :], out.at[at, :], sems.at[k]))
        copies[-1].start()
    full = texts[...].astype(f32)
    inv = lax.rsqrt(jnp.sum(full * full, axis=1, keepdims=True) + eps)
    d_txt = scale[0:1, 0:1] * (own[...] + received[...])
    inner = jnp.sum(full * d_txt, axis=1, keepdims=True)
    text_held[...] = (inv * (d_txt - full * (inv * inv * inner))).astype(bf16)
    copies.append(pltpu.make_async_copy(text_held, text_out, sems.at[len(sizes)]))
    copies[-1].start()
    for copy in copies:
        copy.wait()


def gathered(n_img, n_txt, images, texts, head_weight, log_scale, logit_bias):
    rows, emb = images.shape
    features = texts.shape[1]
    img_at, txt_at = lax.axis_index("img"), lax.axis_index("txt")

    def move(array, axis, mask):
        size = n_img if axis == "img" else n_txt
        return lax.ppermute(array, axis, [(i, i ^ mask) for i in range(size)])

    core = functools.partial(move, axis="img", mask=1)

    def link(array, second):
        pairs = []
        for i in range(n_img):
            for t in range(n_txt):
                to = (i ^ 2) * n_txt + t if (i % 2 == 0) != second else i * n_txt + (t ^ 1)
                pairs.append((i * n_txt + t, to))
        return lax.ppermute(array, ("img", "txt"), pairs)

    def over_z(block):
        return [move(block, "txt", mask) for mask in (2, 4, 6)]

    def shape(count, like):
        return jax.ShapeDtypeStruct((count, like.shape[1]), bf16)

    def after(array, *others):
        return lax.optimization_barrier((array, *others))[0]

    def join(*parts, flops=0):
        count = sum(part.shape[0] for part in parts)
        return call(join_body, shape(count, parts[0]), [VMEM] * len(parts), flops)(*parts)

    far = range(2, n_txt, 2)
    both = ((0, 0), (1, 0), (0, 1), (1, 1))
    order = [(z, *over) for over in both for z in (0, *far)]
    early_order = [(0, *over) for over in both] + [(z, *over) for over in both[:2] for z in far]
    late_order = [(z, *over) for over in both[2:] for z in far]
    total = len(order) * rows
    split = len(early_order) * rows
    first = 2 - lax.rem(img_at, 2)
    place = jnp.stack([img_at, txt_at, first, 3 - first]).astype(jnp.int32)
    txt_z = over_z(texts)
    vector = jax.ShapeDtypeStruct((1, 128), f32)
    txt_own_block, img_own_block, scale, bias = call(
        begin_body,
        [shape(rows, texts), shape(rows, images), vector, vector],
        [SMEM, SMEM, VMEM, VMEM, ANY],
        0,
    )(log_scale, logit_bias, texts, images, txt_z[0])
    img_near = link(images, False)
    img_z = over_z(after(images, txt_z[0]))
    four = join(txt_own_block, *txt_z[:2], after(txt_z[2], img_near))
    got = link(four, False)
    two = join(img_own_block, img_near)
    img_two = link(two, True)
    half = join(four, after(got, img_two))
    got = link(half, True)
    third = total // 3
    *txt_parts, txt_own, col_ids = call(
        functools.partial(unit_body, order, n_img),
        [shape(third, texts)] * 3 + [shape(total, texts), jax.ShapeDtypeStruct((1, 2 * total), jnp.int32)],
        [SMEM] + [VMEM] * 2,
        0,
    )(place, half, got)
    txt_sib = join(*[core(part) for part in txt_parts])
    three = join(*img_z[:2], img_z[2], flops=0)
    six = join(three, link(three, False))
    img_last = [link(six, True)]
    early = [join(two, img_two, six)]
    early_sib = [core(part) for part in early]

    def batch(images, order, cost, before):
        held = images.shape[0]
        term = jax.ShapeDtypeStruct((rows, features), f32)
        return call(
            functools.partial(batch_body, not before, order, n_txt),
            [shape(held, texts), term, term],
            [SMEM] + [VMEM] * (7 + len(before)),
            cost,
            [
                pltpu.VMEM((held, features), f32),
                pltpu.VMEM((held, features), bf16),
                pltpu.VMEM((held, 2 * total), bf16),
            ],
        )(place, scale, bias, images, head_weight, txt_own, txt_sib, col_ids, *before)

    d_early, own, sib = batch(early[0], early_order, 3_000_000_000, [])
    d_early_sib = core(d_early)
    late_sib = [core(after(part, d_early)) for part in img_last]
    d_late, own, sib = batch(img_last[0], late_order, 6_000_000_000, [own, sib])
    d_late_sib = core(d_late)
    received = core(sib)

    left = early + early_sib
    right = [d_early, d_early_sib]
    head = jax.ShapeDtypeStruct((emb, features), f32)
    before, image_grads = call(
        functools.partial(head_early_body, len(left)),
        [head, shape(rows, images)],
        [VMEM] * (1 + len(left) + len(right)),
        0,
    )(head_weight, *left, *right)
    left = img_last + late_sib
    right = [d_late, d_late_sib]
    sizes = [256, 384, emb - 640] if emb % 128 == 0 and emb > 640 else [emb]
    head_grad, text_grads = pl.pallas_call(
        functools.partial(last_body, len(left), len(right), sizes),
        out_shape=[head, shape(rows, texts)],
        in_specs=[VMEM] * (len(left) + len(right) + 5),
        out_specs=[ANY, ANY],
        scratch_shapes=[
            pltpu.VMEM(head.shape, f32),
            pltpu.VMEM(texts.shape, bf16),
            pltpu.SemaphoreType.DMA((len(sizes) + 1,)),
        ],
        compiler_params=pltpu.CompilerParams(vmem_limit_bytes=LIMIT),
        cost_estimate=pl.CostEstimate(flops=0, bytes_accessed=0, transcendentals=0),
    )(scale, txt_own_block, own, received, *left, *right, before)
    return image_grads, text_grads, head_grad


def blocked(images, texts, head_weight, log_scale, logit_bias):
    scale = jnp.exp(log_scale[0])
    bias = logit_bias[0]
    hidden = jnp.dot(images, head_weight, preferred_element_type=f32)
    img_inv = lax.rsqrt(jnp.sum(hidden * hidden, axis=1, keepdims=True) + eps)
    img_unit = (hidden * img_inv).astype(bf16)
    txt_full = texts.astype(f32)
    txt_inv = lax.rsqrt(jnp.sum(txt_full * txt_full, axis=1, keepdims=True) + eps)
    txt_unit = (txt_full * txt_inv).astype(bf16)
    img_block = lax.all_gather(img_unit, "txt", axis=0, tiled=True)
    txt_block = lax.all_gather(txt_unit, "img", axis=0, tiled=True)
    total_rows = img_block.shape[0]
    total_cols = txt_block.shape[0]
    features = img_block.shape[1]
    row_first = lax.axis_index("img") * total_rows
    col_first = lax.axis_index("txt") * total_cols
    columns = col_first + jnp.arange(total_cols, dtype=jnp.int32)
    width = 512 if total_rows % 512 == 0 else total_rows
    count = total_rows // width
    blocks = img_block.reshape(count, width, features)

    def step(carry, inputs):
        block, index = inputs
        logits = scale * dot(block, txt_block, NT) + bias
        row_ids = row_first + index * width + jnp.arange(width, dtype=jnp.int32)
        label = jnp.where(row_ids[:, None] == columns[None, :], 1.0, -1.0).astype(f32)
        grad = (-label * jax.nn.sigmoid(-label * logits)).astype(bf16)
        d_rows = scale * dot(grad, txt_block)
        carry = carry + scale * dot(grad, block, TN)
        return (carry, d_rows)

    txt_terms, row_terms = lax.scan(
        step,
        jnp.zeros((total_cols, features), f32),
        (blocks, jnp.arange(count, dtype=jnp.int32)),
    )
    img_terms = row_terms.reshape(total_rows, features)
    d_img = lax.psum_scatter(
        img_terms.astype(bf16), "txt", scatter_dimension=0, tiled=True
    ).astype(f32)
    inner = jnp.sum(hidden * d_img, axis=1, keepdims=True)
    d_hidden = (img_inv * (d_img - hidden * img_inv * img_inv * inner)).astype(bf16)
    image_grads = dot(d_hidden, head_weight, NT).astype(bf16)
    head_grad = lax.psum(dot(images, d_hidden, TN), ("img", "txt"))
    d_txt = lax.psum_scatter(
        txt_terms.astype(bf16), "img", scatter_dimension=0, tiled=True
    ).astype(f32)
    inner_txt = jnp.sum(txt_full * d_txt, axis=1, keepdims=True)
    text_grads = (txt_inv * (d_txt - txt_full * txt_inv * txt_inv * inner_txt)).astype(bf16)
    return (image_grads, text_grads, head_grad)


def solution(mesh):
    n_img, n_txt = mesh.shape["img"], mesh.shape["txt"]

    def shards(images, texts, head_weight, log_scale, logit_bias):
        width = images.shape[1] + texts.shape[1]
        held = 2 * n_img * n_txt * images.shape[0] * width
        same = images.shape[0] == texts.shape[0]
        if (n_img, n_txt) == (4, 8) and same and held <= GATHER_BYTES:
            return gathered(n_img, n_txt, images, texts, head_weight, log_scale, logit_bias)
        return blocked(images, texts, head_weight, log_scale, logit_bias)

    return jax.shard_map(
        shards,
        mesh=mesh,
        in_specs=(P(("img", "txt"), None), P(("txt", "img"), None), P(), P(), P()),
        out_specs=(P(("img", "txt"), None), P(("txt", "img"), None), P()),
        check_vma=False,
    )
```

```python
import functools

import jax
import jax.numpy as jnp
import numpy as np
from jax import lax
from jax.experimental import pallas as pl
from jax.experimental.pallas import tpu as pltpu
from jax.sharding import PartitionSpec as P

eps = 1e-06
f32, bf16 = jnp.float32, jnp.bfloat16
NT = (((1,), (1,)), ((), ()))
TN = (((0,), (0,)), ((), ()))
VMEM = pl.BlockSpec(memory_space=pltpu.VMEM)
ANY = pl.BlockSpec(memory_space=pl.ANY)
SMEM = pl.BlockSpec(memory_space=pltpu.SMEM)
LIMIT = 32 * 1024 * 1024
GATHER_BYTES = 8 * 1024 * 1024


def dot(a, b, dims=(((1,), (0,)), ((), ()))):
    return lax.dot_general(a, b, dims, preferred_element_type=f32)


def call(body, out_shape, in_specs, flops, scratch=()):
    return pl.pallas_call(
        body,
        out_shape=out_shape,
        in_specs=in_specs,
        out_specs=jax.tree.map(lambda _: VMEM, out_shape),
        scratch_shapes=scratch,
        compiler_params=pltpu.CompilerParams(vmem_limit_bytes=LIMIT),
        cost_estimate=pl.CostEstimate(flops=flops, bytes_accessed=0, transcendentals=0),
    )


def source(place, side, entry):
    z, first, second = entry
    over = (place[2], place[3]) if side == 0 else (place[3], place[2])
    mask = first * over[0] + second * over[1]
    return place[0] ^ (2 * (mask // 2)), place[1] ^ z ^ lax.rem(mask, 2)


def unit_body(order, n_img, place, *refs):
    parts, sent, whole, ids = refs[:4], refs[4:-2], refs[-2], refs[-1]
    total, rows = whole.shape[0], parts[0].shape[0]
    block = total // len(order)
    lane = lax.broadcasted_iota(jnp.int32, ids.shape, 1)
    found = jnp.zeros(ids.shape, jnp.int32)
    for k, entry in enumerate(order):
        for side in (0, 1):
            img, txt = source(place, side, entry)
            first_id = (txt * n_img + (img ^ side)) * block
            at = side * total + k * block
            here = jnp.logical_and(lane >= at, lane < at + block)
            found = jnp.where(here, first_id - at + lane, found)
    ids[...] = found
    size = sent[0].shape[0]
    step = 64
    for at in range(0, total, step):
        full = parts[at // rows][pl.ds(at % rows, step), :].astype(f32)
        inv = lax.rsqrt(jnp.sum(full * full, axis=1, keepdims=True) + eps)
        unit = (full * inv).astype(bf16)
        whole[pl.ds(at, step), :] = unit
        sent[at // size][pl.ds(at % size, step), :] = unit


def batch_body(first, order, n_txt, place, scale_ref, bias_ref, images, weight, txt_own, txt_sib, col_ids, *refs):
    if first:
        d_hidden_ref, own_ref, sib_ref, hidden_ref, unit_ref, grad_ref = refs
    else:
        own_in, sib_in, d_hidden_ref, own_ref, sib_ref, hidden_ref, unit_ref, grad_ref = refs
    scale, bias = scale_ref[0:1, 0:1], bias_ref[0:1, 0:1]
    block = own_ref.shape[0]
    hidden = dot(images[...], weight[...])
    inv = lax.rsqrt(jnp.sum(hidden * hidden, axis=1, keepdims=True) + eps)
    hidden_ref[...] = hidden
    unit_ref[...] = (hidden * inv).astype(bf16)
    ids = []
    for entry in order:
        img, txt = source(place, 0, entry)
        within = lax.broadcasted_iota(jnp.int32, (block, 1), 0)
        ids.append((img * n_txt + txt) * block + within)
    ids = jnp.concatenate(ids, axis=0)
    total = txt_own.shape[0]
    width = 256 if total % 256 == 0 else total
    for side, txt in enumerate((txt_own, txt_sib)):
        for at in range(0, total, width):
            columns = pl.ds(side * total + at, width)
            logits = scale * dot(unit_ref[...], txt[pl.ds(at, width), :], NT) + bias
            flip = jnp.where(ids == col_ids[:, columns], -1.0, 1.0)
            grad_ref[:, columns] = (flip * jax.nn.sigmoid(flip * logits)).astype(bf16)
    edge = 64
    both = jnp.concatenate([grad_ref[:, pl.ds(at, edge)] for at in (0, total)], axis=1)
    terms = dot(both, unit_ref[...], TN)
    for at, ref in ((0, own_ref), (edge, sib_ref)):
        ref[...] = terms[at : at + block, :]
    if not first:
        own_ref[...] += own_in[...]
        sib_ref[...] += sib_in[...]
    d_img = dot(grad_ref[:, pl.ds(0, total)], txt_own[...])
    d_img = scale * (d_img + dot(grad_ref[:, pl.ds(total, total)], txt_sib[...]))
    hidden = hidden_ref[...]
    inner = jnp.sum(hidden * d_img, axis=1, keepdims=True)
    d_hidden_ref[...] = (inv * (d_img - hidden * (inv * inv * inner))).astype(bf16)


def begin_body(log_scale, logit_bias, texts, images, _, texts_out, images_out, scale, bias):
    scale[...] = jnp.exp(jnp.full(scale.shape, log_scale[0], f32))
    bias[...] = jnp.full(bias.shape, logit_bias[0], f32)
    texts_out[...] = texts[...]
    images_out[...] = images[...]


def hold_body(array, _, out, sem):
    copy = pltpu.make_async_copy(array, out, sem)
    copy.start()
    copy.wait()


def join_body(*refs):
    out, at = refs[-1], 0
    for ref in refs[:-1]:
        out[pl.ds(at, ref.shape[0]), :] = ref[...]
        at += ref.shape[0]


def head_early_body(count, *refs):
    images, d_hidden, out = refs[:count], refs[count:-1], refs[-1]
    left = jnp.concatenate([ref[...] for ref in images], axis=0)
    right = jnp.concatenate([ref[...] for ref in d_hidden], axis=0)
    out[...] = dot(left, right, TN)


def last_body(count, d_count, sizes, scale, texts, own, received, weight, mine, *refs):
    images, d_hidden = refs[:count], refs[count : count + d_count]
    before, out, text_out, img_out, held, text_held, img_held, sems = refs[count + d_count :]
    right = jnp.concatenate([ref[...] for ref in d_hidden], axis=0)
    copies = []
    first = 0
    for k, size in enumerate(sizes):
        at = pl.ds(first, size)
        first += size
        left = jnp.concatenate([ref[:, at] for ref in images], axis=0)
        held[at, :] = before[at, :] + dot(left, right, TN)
        copies.append(pltpu.make_async_copy(held.at[at, :], out.at[at, :], sems.at[k]))
        copies[-1].start()
    full = texts[...].astype(f32)
    inv = lax.rsqrt(jnp.sum(full * full, axis=1, keepdims=True) + eps)
    d_txt = scale[0:1, 0:1] * (own[...] + received[...])
    inner = jnp.sum(full * d_txt, axis=1, keepdims=True)
    text_held[...] = (inv * (d_txt - full * (inv * inv * inner))).astype(bf16)
    copies.append(pltpu.make_async_copy(text_held, text_out, sems.at[len(sizes)]))
    copies[-1].start()
    block = mine[pl.ds(0, img_held.shape[0]), :]
    img_held[...] = dot(weight[...], block, NT).T.astype(bf16)
    copies.append(pltpu.make_async_copy(img_held, img_out, sems.at[len(sizes) + 1]))
    copies[-1].start()
    for copy in copies:
        copy.wait()


def gathered(n_img, n_txt, images, texts, head_weight, log_scale, logit_bias):
    rows, emb = images.shape
    features = texts.shape[1]
    img_at, txt_at = lax.axis_index("img"), lax.axis_index("txt")

    def move(array, axis, mask):
        size = n_img if axis == "img" else n_txt
        return lax.ppermute(array, axis, [(i, i ^ mask) for i in range(size)])

    core = functools.partial(move, axis="img", mask=1)

    def link(array, second):
        pairs = []
        for i in range(n_img):
            for t in range(n_txt):
                to = (i ^ 2) * n_txt + t if (i % 2 == 0) != second else i * n_txt + (t ^ 1)
                pairs.append((i * n_txt + t, to))
        return lax.ppermute(array, ("img", "txt"), pairs)

    def over_z(block):
        return [move(block, "txt", mask) for mask in (2, 4, 6)]

    def shape(count, like):
        return jax.ShapeDtypeStruct((count, like.shape[1]), bf16)

    def after(array, *others):
        return lax.optimization_barrier((array, *others))[0]

    def join(*parts, flops=0):
        count = sum(part.shape[0] for part in parts)
        return call(join_body, shape(count, parts[0]), [VMEM] * len(parts), flops)(*parts)

    far = range(2, n_txt, 2)
    both = ((0, 0), (1, 0), (0, 1), (1, 1))
    order = [(z, *over) for over in both for z in (0, *far)]
    early_order = [(0, *over) for over in both] + [(z, *over) for over in both[:2] for z in far]
    late_order = [(z, *over) for over in both[2:] for z in far]
    total = len(order) * rows
    split = len(early_order) * rows
    first = 2 - lax.rem(img_at, 2)
    place = jnp.stack([img_at, txt_at, first, 3 - first]).astype(jnp.int32)
    txt_z = over_z(texts)
    vector = jax.ShapeDtypeStruct((1, 128), f32)
    txt_own_block, img_own_block, scale, bias = call(
        begin_body,
        [shape(rows, texts), shape(rows, images), vector, vector],
        [SMEM, SMEM, VMEM, VMEM, ANY],
        0,
    )(log_scale, logit_bias, texts, images, txt_z[0])
    img_near = link(images, False)
    img_z = over_z(after(images, txt_z[0]))
    four = join(txt_own_block, *txt_z[:2], after(txt_z[2], img_near))
    near = link(four, False)
    far = link(four, True)
    two = join(img_own_block, img_near)
    img_two = link(two, True)
    txt_parts = [four, near, far, link(after(near, *(img_two,)), True)]
    third = total // 3
    *sent, txt_own, col_ids = call(
        functools.partial(unit_body, order, n_img),
        [shape(third, texts)] * 3 + [shape(total, texts), jax.ShapeDtypeStruct((1, 2 * total), jnp.int32)],
        [SMEM] + [VMEM] * len(txt_parts),
        0,
    )(place, *txt_parts)
    txt_sib = join(*[core(part) for part in sent])
    weight = call(hold_body, jax.ShapeDtypeStruct(head_weight.shape, bf16), [ANY, ANY], 0, [
        pltpu.SemaphoreType.DMA
    ])(head_weight, img_two)
    three = join(*img_z[:2], after(img_z[2], weight), flops=0)
    near = link(three, False)
    far = link(three, True)
    early = [join(two, img_two, three, near)]
    img_last = [join(far, link(after(near, *()), True))]
    early_sib = [core(part) for part in early]

    def batch(images, order, cost, before):
        held = images.shape[0]
        term = jax.ShapeDtypeStruct((rows, features), f32)
        return call(
            functools.partial(batch_body, not before, order, n_txt),
            [shape(held, texts), term, term],
            [SMEM] + [VMEM] * (7 + len(before)),
            cost,
            [
                pltpu.VMEM((held, features), f32),
                pltpu.VMEM((held, features), bf16),
                pltpu.VMEM((held, 2 * total), bf16),
            ],
        )(place, scale, bias, images, weight, txt_own, txt_sib, col_ids, *before)

    d_early, own, sib = batch(early[0], early_order, 1_400_000_000, [])
    d_early_sib = core(d_early)
    late_sib = [core(after(part, d_early)) for part in img_last]
    d_late, own, sib = batch(img_last[0], late_order, 6_000_000_000, [own, sib])
    d_late_sib = core(d_late)
    received = core(sib)

    left = early + early_sib
    right = [d_early, d_early_sib]
    head = jax.ShapeDtypeStruct((emb, features), f32)
    before = call(
        functools.partial(head_early_body, len(left)),
        head,
        [VMEM] * (len(left) + len(right)),
        0,
    )(*left, *right)
    left = img_last + late_sib
    right = [d_late, d_late_sib]
    sizes = [256, 384, emb - 640] if emb % 128 == 0 and emb > 640 else [emb]
    head_grad, text_grads, image_grads = pl.pallas_call(
        functools.partial(last_body, len(left), len(right), sizes),
        out_shape=[head, shape(rows, texts), shape(rows, images)],
        in_specs=[VMEM] * (len(left) + len(right) + 7),
        out_specs=[ANY] * 3,
        scratch_shapes=[
            pltpu.VMEM(head.shape, f32),
            pltpu.VMEM(texts.shape, bf16),
            pltpu.VMEM(images.shape, bf16),
            pltpu.SemaphoreType.DMA((len(sizes) + 2,)),
        ],
        compiler_params=pltpu.CompilerParams(vmem_limit_bytes=LIMIT),
        cost_estimate=pl.CostEstimate(flops=0, bytes_accessed=0, transcendentals=0),
    )(scale, txt_own_block, own, received, weight, d_early, *left, *right, before)
    return image_grads, text_grads, head_grad


def blocked(images, texts, head_weight, log_scale, logit_bias):
    scale = jnp.exp(log_scale[0])
    bias = logit_bias[0]
    hidden = jnp.dot(images, head_weight, preferred_element_type=f32)
    img_inv = lax.rsqrt(jnp.sum(hidden * hidden, axis=1, keepdims=True) + eps)
    img_unit = (hidden * img_inv).astype(bf16)
    txt_full = texts.astype(f32)
    txt_inv = lax.rsqrt(jnp.sum(txt_full * txt_full, axis=1, keepdims=True) + eps)
    txt_unit = (txt_full * txt_inv).astype(bf16)
    img_block = lax.all_gather(img_unit, "txt", axis=0, tiled=True)
    txt_block = lax.all_gather(txt_unit, "img", axis=0, tiled=True)
    total_rows = img_block.shape[0]
    total_cols = txt_block.shape[0]
    features = img_block.shape[1]
    row_first = lax.axis_index("img") * total_rows
    col_first = lax.axis_index("txt") * total_cols
    columns = col_first + jnp.arange(total_cols, dtype=jnp.int32)
    width = 512 if total_rows % 512 == 0 else total_rows
    count = total_rows // width
    blocks = img_block.reshape(count, width, features)

    def step(carry, inputs):
        block, index = inputs
        logits = scale * dot(block, txt_block, NT) + bias
        row_ids = row_first + index * width + jnp.arange(width, dtype=jnp.int32)
        label = jnp.where(row_ids[:, None] == columns[None, :], 1.0, -1.0).astype(f32)
        grad = (-label * jax.nn.sigmoid(-label * logits)).astype(bf16)
        d_rows = scale * dot(grad, txt_block)
        carry = carry + scale * dot(grad, block, TN)
        return (carry, d_rows)

    txt_terms, row_terms = lax.scan(
        step,
        jnp.zeros((total_cols, features), f32),
        (blocks, jnp.arange(count, dtype=jnp.int32)),
    )
    img_terms = row_terms.reshape(total_rows, features)
    d_img = lax.psum_scatter(
        img_terms.astype(bf16), "txt", scatter_dimension=0, tiled=True
    ).astype(f32)
    inner = jnp.sum(hidden * d_img, axis=1, keepdims=True)
    d_hidden = (img_inv * (d_img - hidden * img_inv * img_inv * inner)).astype(bf16)
    image_grads = dot(d_hidden, head_weight, NT).astype(bf16)
    head_grad = lax.psum(dot(images, d_hidden, TN), ("img", "txt"))
    d_txt = lax.psum_scatter(
        txt_terms.astype(bf16), "img", scatter_dimension=0, tiled=True
    ).astype(f32)
    inner_txt = jnp.sum(txt_full * d_txt, axis=1, keepdims=True)
    text_grads = (txt_inv * (d_txt - txt_full * txt_inv * txt_inv * inner_txt)).astype(bf16)
    return (image_grads, text_grads, head_grad)


def solution(mesh):
    n_img, n_txt = mesh.shape["img"], mesh.shape["txt"]

    def shards(images, texts, head_weight, log_scale, logit_bias):
        width = images.shape[1] + texts.shape[1]
        held = 2 * n_img * n_txt * images.shape[0] * width
        same = images.shape[0] == texts.shape[0]
        if (n_img, n_txt) == (4, 8) and same and held <= GATHER_BYTES:
            return gathered(n_img, n_txt, images, texts, head_weight, log_scale, logit_bias)
        return blocked(images, texts, head_weight, log_scale, logit_bias)

    return jax.shard_map(
        shards,
        mesh=mesh,
        in_specs=(P(("img", "txt"), None), P(("txt", "img"), None), P(), P(), P()),
        out_specs=(P(("img", "txt"), None), P(("txt", "img"), None), P()),
        check_vma=False,
    )
```

```python
import functools

import jax
import jax.numpy as jnp
import numpy as np
from jax import lax
from jax.experimental import pallas as pl
from jax.experimental.pallas import tpu as pltpu
from jax.sharding import PartitionSpec as P

eps = 1e-06
f32, bf16 = jnp.float32, jnp.bfloat16
NT = (((1,), (1,)), ((), ()))
TN = (((0,), (0,)), ((), ()))
VMEM = pl.BlockSpec(memory_space=pltpu.VMEM)
ANY = pl.BlockSpec(memory_space=pl.ANY)
SMEM = pl.BlockSpec(memory_space=pltpu.SMEM)
LIMIT = 32 * 1024 * 1024
GATHER_BYTES = 8 * 1024 * 1024


def dot(a, b, dims=(((1,), (0,)), ((), ()))):
    return lax.dot_general(a, b, dims, preferred_element_type=f32)


def call(body, out_shape, in_specs, flops, scratch=()):
    return pl.pallas_call(
        body,
        out_shape=out_shape,
        in_specs=in_specs,
        out_specs=jax.tree.map(lambda _: VMEM, out_shape),
        scratch_shapes=scratch,
        compiler_params=pltpu.CompilerParams(vmem_limit_bytes=LIMIT),
        cost_estimate=pl.CostEstimate(flops=flops, bytes_accessed=0, transcendentals=0),
    )


def source(place, side, entry):
    z, first, second = entry
    over = (place[2], place[3]) if side == 0 else (place[3], place[2])
    mask = first * over[0] + second * over[1]
    return place[0] ^ (2 * (mask // 2)), place[1] ^ z ^ lax.rem(mask, 2)


def unit_body(order, n_img, place, _, *refs):
    parts, sent, whole, ids = refs[:4], refs[4:-2], refs[-2], refs[-1]
    total, rows = whole.shape[0], parts[0].shape[0]
    block = total // len(order)
    lane = lax.broadcasted_iota(jnp.int32, ids.shape, 1)
    found = jnp.zeros(ids.shape, jnp.int32)
    for k, entry in enumerate(order):
        for side in (0, 1):
            img, txt = source(place, side, entry)
            first_id = (txt * n_img + (img ^ side)) * block
            at = side * total + k * block
            here = jnp.logical_and(lane >= at, lane < at + block)
            found = jnp.where(here, first_id - at + lane, found)
    ids[...] = found
    size = sent[0].shape[0]
    step = 64
    for at in range(0, total, step):
        full = parts[at // rows][pl.ds(at % rows, step), :].astype(f32)
        inv = lax.rsqrt(jnp.sum(full * full, axis=1, keepdims=True) + eps)
        unit = (full * inv).astype(bf16)
        whole[pl.ds(at, step), :] = unit
        sent[at // size][pl.ds(at % size, step), :] = unit


def hidden_body(images, weight, hidden_out, unit_out, inv_out):
    hidden = dot(images[...], weight[...])
    inv = lax.rsqrt(jnp.sum(hidden * hidden, axis=1, keepdims=True) + eps)
    hidden_out[...] = hidden
    unit_out[...] = (hidden * inv).astype(bf16)
    inv_out[...] = inv


def batch_body(
    first, order, n_txt, place, scale_ref, bias_ref, images, weight, txt_own, txt_sib, col_ids, *refs
):
    if first:
        hidden_in, unit_in, inv_in, d_hidden_ref, own_ref, sib_ref, hidden_ref, unit_ref, grad_ref = refs
    else:
        own_in, sib_in, d_hidden_ref, own_ref, sib_ref, hidden_ref, unit_ref, grad_ref = refs
    scale, bias = scale_ref[0:1, 0:1], bias_ref[0:1, 0:1]
    block = own_ref.shape[0]
    hidden = dot(images[...], weight[...])
    inv = lax.rsqrt(jnp.sum(hidden * hidden, axis=1, keepdims=True) + eps)
    at = hidden_ref.shape[0] - images.shape[0]
    hidden_ref[pl.ds(at, images.shape[0]), :] = hidden
    unit_ref[pl.ds(at, images.shape[0]), :] = (hidden * inv).astype(bf16)
    if first:
        hidden_ref[pl.ds(0, at), :] = hidden_in[...]
        unit_ref[pl.ds(0, at), :] = unit_in[...]
        inv = jnp.concatenate([inv_in[...], inv], axis=0)
    ids = []
    for entry in order:
        img, txt = source(place, 0, entry)
        within = lax.broadcasted_iota(jnp.int32, (block, 1), 0)
        ids.append((img * n_txt + txt) * block + within)
    ids = jnp.concatenate(ids, axis=0)
    total = txt_own.shape[0]
    width = 256 if total % 256 == 0 else total
    for side, txt in enumerate((txt_own, txt_sib)):
        for at in range(0, total, width):
            columns = pl.ds(side * total + at, width)
            logits = scale * dot(unit_ref[...], txt[pl.ds(at, width), :], NT) + bias
            flip = jnp.where(ids == col_ids[:, columns], -1.0, 1.0)
            grad_ref[:, columns] = (flip * jax.nn.sigmoid(flip * logits)).astype(bf16)
    edge = 64
    both = jnp.concatenate([grad_ref[:, pl.ds(at, edge)] for at in (0, total)], axis=1)
    terms = dot(both, unit_ref[...], TN)
    for at, ref in ((0, own_ref), (edge, sib_ref)):
        ref[...] = terms[at : at + block, :]
    if not first:
        own_ref[...] += own_in[...]
        sib_ref[...] += sib_in[...]
    d_img = dot(grad_ref[:, pl.ds(0, total)], txt_own[...])
    d_img = scale * (d_img + dot(grad_ref[:, pl.ds(total, total)], txt_sib[...]))
    hidden = hidden_ref[...]
    inner = jnp.sum(hidden * d_img, axis=1, keepdims=True)
    d_hidden_ref[...] = (inv * (d_img - hidden * (inv * inv * inner))).astype(bf16)


def begin_body(log_scale, logit_bias, texts, images, _, texts_out, images_out, scale, bias):
    scale[...] = jnp.exp(jnp.full(scale.shape, log_scale[0], f32))
    bias[...] = jnp.full(bias.shape, logit_bias[0], f32)
    texts_out[...] = texts[...]
    images_out[...] = images[...]


def hold_body(array, _, out, sem):
    copy = pltpu.make_async_copy(array, out, sem)
    copy.start()
    copy.wait()


def join_body(*refs):
    out, at = refs[-1], 0
    for ref in refs[:-1]:
        out[pl.ds(at, ref.shape[0]), :] = ref[...]
        at += ref.shape[0]


def head_body(count, d_count, *refs):
    images, d_hidden, rest = refs[:count], refs[count : count + d_count], refs[count + d_count :]
    left = jnp.concatenate([ref[...] for ref in images], axis=0)
    right = jnp.concatenate([ref[...] for ref in d_hidden], axis=0)
    terms = dot(left, right, TN)
    rest[-1][...] = terms + rest[0][...] if len(rest) == 2 else terms


def last_body(count, d_count, sizes, scale, texts, own, received, weight, mine, *refs):
    images, d_hidden = refs[:count], refs[count : count + d_count]
    before, out, text_out, img_out, held, text_held, img_held, sems = refs[count + d_count :]
    right = jnp.concatenate([ref[...] for ref in d_hidden], axis=0)
    copies = []
    first = 0
    for k, size in enumerate(sizes):
        at = pl.ds(first, size)
        first += size
        left = jnp.concatenate([ref[:, at] for ref in images], axis=0)
        held[at, :] = before[at, :] + dot(left, right, TN)
        copies.append(pltpu.make_async_copy(held.at[at, :], out.at[at, :], sems.at[k]))
        copies[-1].start()
    full = texts[...].astype(f32)
    inv = lax.rsqrt(jnp.sum(full * full, axis=1, keepdims=True) + eps)
    d_txt = scale[0:1, 0:1] * (own[...] + received[...])
    inner = jnp.sum(full * d_txt, axis=1, keepdims=True)
    text_held[...] = (inv * (d_txt - full * (inv * inv * inner))).astype(bf16)
    copies.append(pltpu.make_async_copy(text_held, text_out, sems.at[len(sizes)]))
    copies[-1].start()
    block = mine[pl.ds(0, img_held.shape[0]), :]
    img_held[...] = dot(weight[...], block, NT).T.astype(bf16)
    copies.append(pltpu.make_async_copy(img_held, img_out, sems.at[len(sizes) + 1]))
    copies[-1].start()
    for copy in copies:
        copy.wait()


def gathered(n_img, n_txt, images, texts, head_weight, log_scale, logit_bias):
    rows, emb = images.shape
    features = texts.shape[1]
    img_at, txt_at = lax.axis_index("img"), lax.axis_index("txt")

    def move(array, axis, mask):
        size = n_img if axis == "img" else n_txt
        return lax.ppermute(array, axis, [(i, i ^ mask) for i in range(size)])

    core = functools.partial(move, axis="img", mask=1)

    def link(array, second):
        pairs = []
        for i in range(n_img):
            for t in range(n_txt):
                to = (i ^ 2) * n_txt + t if (i % 2 == 0) != second else i * n_txt + (t ^ 1)
                pairs.append((i * n_txt + t, to))
        return lax.ppermute(array, ("img", "txt"), pairs)

    def over_z(block):
        return [move(block, "txt", mask) for mask in (2, 4, 6)]

    def shape(count, like):
        return jax.ShapeDtypeStruct((count, like.shape[1]), bf16)

    def after(array, *others):
        return lax.optimization_barrier((array, *others))[0]

    def join(*parts, flops=0):
        count = sum(part.shape[0] for part in parts)
        return call(join_body, shape(count, parts[0]), [VMEM] * len(parts), flops)(*parts)

    far = range(2, n_txt, 2)
    both = ((0, 0), (1, 0), (0, 1), (1, 1))
    order = [(z, *over) for over in both for z in (0, *far)]
    early_order = [(0, *over) for over in both] + [(z, *over) for over in both[:2] for z in far]
    late_order = [(z, *over) for over in both[2:] for z in far]
    total = len(order) * rows
    split = len(early_order) * rows
    first = 2 - lax.rem(img_at, 2)
    place = jnp.stack([img_at, txt_at, first, 3 - first]).astype(jnp.int32)
    txt_z = over_z(texts)
    vector = jax.ShapeDtypeStruct((1, 128), f32)
    txt_own_block, img_own_block, scale, bias = call(
        begin_body,
        [shape(rows, texts), shape(rows, images), vector, vector],
        [SMEM, SMEM, VMEM, VMEM, ANY],
        0,
    )(log_scale, logit_bias, texts, images, txt_z[0])
    img_near = link(images, False)
    img_z = over_z(after(images, txt_z[0]))
    four = join(txt_own_block, *txt_z[:2], after(txt_z[2], img_near))
    near = link(four, False)
    far = link(four, True)
    two = join(img_own_block, img_near)
    img_two = link(two, True)
    txt_parts = [four, near, far, link(after(near, *(img_two,)), True)]
    weight = call(hold_body, jax.ShapeDtypeStruct(head_weight.shape, bf16), [ANY, ANY], 0, [
        pltpu.SemaphoreType.DMA
    ])(head_weight, img_two)
    three = join(*img_z[:2], after(img_z[2], weight), flops=1_000_000_000)
    near = link(three, False)
    far = link(three, True)
    ready = join(two, img_two, three)
    ready_hidden = call(
        hidden_body,
        [
            jax.ShapeDtypeStruct((ready.shape[0], features), f32),
            shape(ready.shape[0], texts),
            jax.ShapeDtypeStruct((ready.shape[0], 1), f32),
        ],
        [VMEM] * 2,
        0,
    )(ready, weight)
    third = total // 3
    *sent, txt_own, col_ids = call(
        functools.partial(unit_body, order, n_img),
        [shape(third, texts)] * 3 + [shape(total, texts), jax.ShapeDtypeStruct((1, 2 * total), jnp.int32)],
        [SMEM, ANY] + [VMEM] * len(txt_parts),
        0,
    )(place, ready_hidden[2], *txt_parts)
    txt_sib = join(*[core(part) for part in sent])
    early = [ready, near]
    last = link(near, True)

    def batch(images, order, cost, before):
        held = len(order) * rows
        first = held > images.shape[0]
        term = jax.ShapeDtypeStruct((rows, features), f32)
        return call(
            functools.partial(batch_body, first, order, n_txt),
            [shape(held, texts), term, term],
            [SMEM] + [VMEM] * (7 + len(before)),
            cost,
            [
                pltpu.VMEM((held, features), f32),
                pltpu.VMEM((held, features), bf16),
                pltpu.VMEM((held, 2 * total), bf16),
            ],
        )(place, scale, bias, images, weight, txt_own, txt_sib, col_ids, *before)

    d_early, own, sib = batch(near, early_order, 1_400_000_000, ready_hidden)
    d_early_sib = core(d_early)
    early_sib = [core(ready), core(near)]
    head = jax.ShapeDtypeStruct((emb, features), f32)

    def head_terms(images, d_hidden, *before):
        refs = [*images, *d_hidden, *before]
        body = functools.partial(head_body, len(images), len(d_hidden))
        return call(body, head, [VMEM] * len(refs), 0)(*refs)

    before = head_terms(early, [d_early])
    img_last = [join(after(far, before, early_sib[1]), last)]
    late_sib = [core(part) for part in img_last]
    d_late, own, sib = batch(img_last[0], late_order, 6_000_000_000, [own, sib])
    d_late_sib = core(d_late)
    received = core(sib)

    before = head_terms(early_sib, [d_early_sib], before)
    left = img_last + late_sib
    right = [d_late, d_late_sib]
    sizes = [256, 384, emb - 640] if emb % 128 == 0 and emb > 640 else [emb]
    head_grad, text_grads, image_grads = pl.pallas_call(
        functools.partial(last_body, len(left), len(right), sizes),
        out_shape=[head, shape(rows, texts), shape(rows, images)],
        in_specs=[VMEM] * (len(left) + len(right) + 7),
        out_specs=[ANY] * 3,
        scratch_shapes=[
            pltpu.VMEM(head.shape, f32),
            pltpu.VMEM(texts.shape, bf16),
            pltpu.VMEM(images.shape, bf16),
            pltpu.SemaphoreType.DMA((len(sizes) + 2,)),
        ],
        compiler_params=pltpu.CompilerParams(vmem_limit_bytes=LIMIT),
        cost_estimate=pl.CostEstimate(flops=0, bytes_accessed=0, transcendentals=0),
    )(scale, txt_own_block, own, received, weight, d_early, *left, *right, before)
    return image_grads, text_grads, head_grad


def blocked(images, texts, head_weight, log_scale, logit_bias):
    scale = jnp.exp(log_scale[0])
    bias = logit_bias[0]
    hidden = jnp.dot(images, head_weight, preferred_element_type=f32)
    img_inv = lax.rsqrt(jnp.sum(hidden * hidden, axis=1, keepdims=True) + eps)
    img_unit = (hidden * img_inv).astype(bf16)
    txt_full = texts.astype(f32)
    txt_inv = lax.rsqrt(jnp.sum(txt_full * txt_full, axis=1, keepdims=True) + eps)
    txt_unit = (txt_full * txt_inv).astype(bf16)
    img_block = lax.all_gather(img_unit, "txt", axis=0, tiled=True)
    txt_block = lax.all_gather(txt_unit, "img", axis=0, tiled=True)
    total_rows = img_block.shape[0]
    total_cols = txt_block.shape[0]
    features = img_block.shape[1]
    row_first = lax.axis_index("img") * total_rows
    col_first = lax.axis_index("txt") * total_cols
    columns = col_first + jnp.arange(total_cols, dtype=jnp.int32)
    width = 512 if total_rows % 512 == 0 else total_rows
    count = total_rows // width
    blocks = img_block.reshape(count, width, features)

    def step(carry, inputs):
        block, index = inputs
        logits = scale * dot(block, txt_block, NT) + bias
        row_ids = row_first + index * width + jnp.arange(width, dtype=jnp.int32)
        label = jnp.where(row_ids[:, None] == columns[None, :], 1.0, -1.0).astype(f32)
        grad = (-label * jax.nn.sigmoid(-label * logits)).astype(bf16)
        d_rows = scale * dot(grad, txt_block)
        carry = carry + scale * dot(grad, block, TN)
        return (carry, d_rows)

    txt_terms, row_terms = lax.scan(
        step,
        jnp.zeros((total_cols, features), f32),
        (blocks, jnp.arange(count, dtype=jnp.int32)),
    )
    img_terms = row_terms.reshape(total_rows, features)
    d_img = lax.psum_scatter(
        img_terms.astype(bf16), "txt", scatter_dimension=0, tiled=True
    ).astype(f32)
    inner = jnp.sum(hidden * d_img, axis=1, keepdims=True)
    d_hidden = (img_inv * (d_img - hidden * img_inv * img_inv * inner)).astype(bf16)
    image_grads = dot(d_hidden, head_weight, NT).astype(bf16)
    head_grad = lax.psum(dot(images, d_hidden, TN), ("img", "txt"))
    d_txt = lax.psum_scatter(
        txt_terms.astype(bf16), "img", scatter_dimension=0, tiled=True
    ).astype(f32)
    inner_txt = jnp.sum(txt_full * d_txt, axis=1, keepdims=True)
    text_grads = (txt_inv * (d_txt - txt_full * txt_inv * txt_inv * inner_txt)).astype(bf16)
    return (image_grads, text_grads, head_grad)


def solution(mesh):
    n_img, n_txt = mesh.shape["img"], mesh.shape["txt"]

    def shards(images, texts, head_weight, log_scale, logit_bias):
        width = images.shape[1] + texts.shape[1]
        held = 2 * n_img * n_txt * images.shape[0] * width
        same = images.shape[0] == texts.shape[0]
        if (n_img, n_txt) == (4, 8) and same and held <= GATHER_BYTES:
            return gathered(n_img, n_txt, images, texts, head_weight, log_scale, logit_bias)
        return blocked(images, texts, head_weight, log_scale, logit_bias)

    return jax.shard_map(
        shards,
        mesh=mesh,
        in_specs=(P(("img", "txt"), None), P(("txt", "img"), None), P(), P(), P()),
        out_specs=(P(("img", "txt"), None), P(("txt", "img"), None), P()),
        check_vma=False,
    )
```

```python
import functools

import jax
import jax.numpy as jnp
import numpy as np
from jax import lax
from jax.experimental import pallas as pl
from jax.experimental.pallas import tpu as pltpu
from jax.sharding import PartitionSpec as P

eps = 1e-06
f32, bf16 = jnp.float32, jnp.bfloat16
NT = (((1,), (1,)), ((), ()))
TN = (((0,), (0,)), ((), ()))
VMEM = pl.BlockSpec(memory_space=pltpu.VMEM)
ANY = pl.BlockSpec(memory_space=pl.ANY)
SMEM = pl.BlockSpec(memory_space=pltpu.SMEM)
LIMIT = 32 * 1024 * 1024
GATHER_BYTES = 8 * 1024 * 1024


def dot(a, b, dims=(((1,), (0,)), ((), ()))):
    return lax.dot_general(a, b, dims, preferred_element_type=f32)


def call(body, out_shape, in_specs, flops, scratch=()):
    return pl.pallas_call(
        body,
        out_shape=out_shape,
        in_specs=in_specs,
        out_specs=jax.tree.map(lambda _: VMEM, out_shape),
        scratch_shapes=scratch,
        compiler_params=pltpu.CompilerParams(vmem_limit_bytes=LIMIT),
        cost_estimate=pl.CostEstimate(flops=flops, bytes_accessed=0, transcendentals=0),
    )


def source(place, side, entry):
    z, first, second = entry
    over = (place[2], place[3]) if side == 0 else (place[3], place[2])
    mask = first * over[0] + second * over[1]
    return place[0] ^ (2 * (mask // 2)), place[1] ^ z ^ lax.rem(mask, 2)


def unit_body(order, n_img, place, _, *refs):
    parts, sent, whole, ids = refs[:4], refs[4:-2], refs[-2], refs[-1]
    total, rows = whole.shape[0], parts[0].shape[0]
    block = total // len(order)
    lane = lax.broadcasted_iota(jnp.int32, ids.shape, 1)
    found = jnp.zeros(ids.shape, jnp.int32)
    for k, entry in enumerate(order):
        for side in (0, 1):
            img, txt = source(place, side, entry)
            first_id = (txt * n_img + (img ^ side)) * block
            at = side * total + k * block
            here = jnp.logical_and(lane >= at, lane < at + block)
            found = jnp.where(here, first_id - at + lane, found)
    ids[...] = found
    size = sent[0].shape[0]
    step = 64
    for at in range(0, total, step):
        full = parts[at // rows][pl.ds(at % rows, step), :].astype(f32)
        inv = lax.rsqrt(jnp.sum(full * full, axis=1, keepdims=True) + eps)
        unit = (full * inv).astype(bf16)
        whole[pl.ds(at, step), :] = unit
        sent[at // size][pl.ds(at % size, step), :] = unit


def hidden_body(images, weight, hidden_out, unit_out, inv_out):
    hidden = dot(images[...], weight[...])
    inv = lax.rsqrt(jnp.sum(hidden * hidden, axis=1, keepdims=True) + eps)
    hidden_out[...] = hidden
    unit_out[...] = (hidden * inv).astype(bf16)
    inv_out[...] = inv


def batch_body(
    first, order, n_txt, place, scale_ref, bias_ref, images, weight, txt_own, txt_sib, col_ids, *refs
):
    if first:
        hidden_in, unit_in, inv_in, d_hidden_ref, own_ref, sib_ref, hidden_ref, unit_ref, grad_ref = refs
    else:
        own_in, sib_in, d_hidden_ref, own_ref, sib_ref, hidden_ref, unit_ref, grad_ref = refs
    scale, bias = scale_ref[0:1, 0:1], bias_ref[0:1, 0:1]
    block = own_ref.shape[0]
    hidden = dot(images[...], weight[...])
    inv = lax.rsqrt(jnp.sum(hidden * hidden, axis=1, keepdims=True) + eps)
    at = hidden_ref.shape[0] - images.shape[0]
    hidden_ref[pl.ds(at, images.shape[0]), :] = hidden
    unit_ref[pl.ds(at, images.shape[0]), :] = (hidden * inv).astype(bf16)
    if first:
        hidden_ref[pl.ds(0, at), :] = hidden_in[...]
        unit_ref[pl.ds(0, at), :] = unit_in[...]
        inv = jnp.concatenate([inv_in[...], inv], axis=0)
    ids = []
    for entry in order:
        img, txt = source(place, 0, entry)
        within = lax.broadcasted_iota(jnp.int32, (block, 1), 0)
        ids.append((img * n_txt + txt) * block + within)
    ids = jnp.concatenate(ids, axis=0)
    total = txt_own.shape[0]
    width = 256 if total % 256 == 0 else total
    for side, txt in enumerate((txt_own, txt_sib)):
        for at in range(0, total, width):
            columns = pl.ds(side * total + at, width)
            logits = scale * dot(unit_ref[...], txt[pl.ds(at, width), :], NT) + bias
            flip = jnp.where(ids == col_ids[:, columns], -1.0, 1.0)
            grad_ref[:, columns] = (flip * jax.nn.sigmoid(flip * logits)).astype(bf16)
    edge = 64
    both = jnp.concatenate([grad_ref[:, pl.ds(at, edge)] for at in (0, total)], axis=1)
    terms = dot(both, unit_ref[...], TN)
    for at, ref in ((0, own_ref), (edge, sib_ref)):
        ref[...] = terms[at : at + block, :]
    if not first:
        own_ref[...] += own_in[...]
        sib_ref[...] += sib_in[...]
    d_img = dot(grad_ref[:, pl.ds(0, total)], txt_own[...])
    d_img = scale * (d_img + dot(grad_ref[:, pl.ds(total, total)], txt_sib[...]))
    hidden = hidden_ref[...]
    inner = jnp.sum(hidden * d_img, axis=1, keepdims=True)
    d_hidden_ref[...] = (inv * (d_img - hidden * (inv * inv * inner))).astype(bf16)


def begin_body(log_scale, logit_bias, texts, images, _, texts_out, images_out, scale, bias):
    scale[...] = jnp.exp(jnp.full(scale.shape, log_scale[0], f32))
    bias[...] = jnp.full(bias.shape, logit_bias[0], f32)
    texts_out[...] = texts[...]
    images_out[...] = images[...]


def hold_body(array, _, out, sem):
    copy = pltpu.make_async_copy(array, out, sem)
    copy.start()
    copy.wait()


def join_body(*refs):
    out, at = refs[-1], 0
    for ref in refs[:-1]:
        out[pl.ds(at, ref.shape[0]), :] = ref[...]
        at += ref.shape[0]


def head_body(count, d_count, *refs):
    images, d_hidden, rest = refs[:count], refs[count : count + d_count], refs[count + d_count :]
    left = jnp.concatenate([ref[...] for ref in images], axis=0)
    right = jnp.concatenate([ref[...] for ref in d_hidden], axis=0)
    terms = dot(left, right, TN)
    rest[-1][...] = terms + rest[0][...] if len(rest) == 2 else terms


def last_body(count, d_count, sizes, scale, texts, own, received, weight, mine, *refs):
    images, d_hidden = refs[:count], refs[count : count + d_count]
    before, out, text_out, img_out, held, text_held, img_held, sems = refs[count + d_count :]
    right = jnp.concatenate([ref[...] for ref in d_hidden], axis=0)
    copies = []
    first = 0
    for k, size in enumerate(sizes):
        at = pl.ds(first, size)
        first += size
        left = jnp.concatenate([ref[:, at] for ref in images], axis=0)
        held[at, :] = before[at, :] + dot(left, right, TN)
        copies.append(pltpu.make_async_copy(held.at[at, :], out.at[at, :], sems.at[k]))
        copies[-1].start()
    full = texts[...].astype(f32)
    inv = lax.rsqrt(jnp.sum(full * full, axis=1, keepdims=True) + eps)
    d_txt = scale[0:1, 0:1] * (own[...] + received[...])
    inner = jnp.sum(full * d_txt, axis=1, keepdims=True)
    text_held[...] = (inv * (d_txt - full * (inv * inv * inner))).astype(bf16)
    copies.append(pltpu.make_async_copy(text_held, text_out, sems.at[len(sizes)]))
    copies[-1].start()
    block = mine[pl.ds(0, img_held.shape[0]), :]
    img_held[...] = dot(weight[...], block, NT).T.astype(bf16)
    copies.append(pltpu.make_async_copy(img_held, img_out, sems.at[len(sizes) + 1]))
    copies[-1].start()
    for copy in copies:
        copy.wait()


def gathered(n_img, n_txt, images, texts, head_weight, log_scale, logit_bias):
    rows, emb = images.shape
    features = texts.shape[1]
    img_at, txt_at = lax.axis_index("img"), lax.axis_index("txt")

    def move(array, axis, mask):
        size = n_img if axis == "img" else n_txt
        return lax.ppermute(array, axis, [(i, i ^ mask) for i in range(size)])

    core = functools.partial(move, axis="img", mask=1)

    def link(array, second):
        pairs = []
        for i in range(n_img):
            for t in range(n_txt):
                to = (i ^ 2) * n_txt + t if (i % 2 == 0) != second else i * n_txt + (t ^ 1)
                pairs.append((i * n_txt + t, to))
        return lax.ppermute(array, ("img", "txt"), pairs)

    def over_z(block):
        return [move(block, "txt", mask) for mask in (2, 4, 6)]

    def shape(count, like):
        return jax.ShapeDtypeStruct((count, like.shape[1]), bf16)

    def after(array, *others):
        return lax.optimization_barrier((array, *others))[0]

    def join(*parts, flops=0):
        count = sum(part.shape[0] for part in parts)
        return call(join_body, shape(count, parts[0]), [VMEM] * len(parts), flops)(*parts)

    far = range(2, n_txt, 2)
    both = ((0, 0), (1, 0), (0, 1), (1, 1))
    order = [(z, *over) for over in both for z in (0, *far)]
    early_order = [(0, *over) for over in both] + [(z, *over) for over in both[:2] for z in far]
    late_order = [(z, *over) for over in both[2:] for z in far]
    total = len(order) * rows
    split = len(early_order) * rows
    first = 2 - lax.rem(img_at, 2)
    place = jnp.stack([img_at, txt_at, first, 3 - first]).astype(jnp.int32)
    txt_z = over_z(texts)
    vector = jax.ShapeDtypeStruct((1, 128), f32)
    txt_own_block, img_own_block, scale, bias = call(
        begin_body,
        [shape(rows, texts), shape(rows, images), vector, vector],
        [SMEM, SMEM, VMEM, VMEM, ANY],
        0,
    )(log_scale, logit_bias, texts, images, txt_z[0])
    img_near = link(images, False)
    img_z = over_z(after(images, txt_z[0]))
    four = join(txt_own_block, *txt_z[:2], after(txt_z[2], img_near))
    near = link(four, False)
    far = link(four, True)
    two = join(img_own_block, img_near)
    img_two = link(two, True)
    txt_parts = [four, near, far, link(after(near, *(img_two,)), True)]
    weight = call(hold_body, jax.ShapeDtypeStruct(head_weight.shape, bf16), [ANY, ANY], 0, [
        pltpu.SemaphoreType.DMA
    ])(head_weight, img_two)
    three = join(*img_z[:2], after(img_z[2], weight), flops=1_000_000_000)
    near = link(three, False)
    far = link(three, True)
    ready = join(two, img_two, three)
    ready_hidden = call(
        hidden_body,
        [
            jax.ShapeDtypeStruct((ready.shape[0], features), f32),
            shape(ready.shape[0], texts),
            jax.ShapeDtypeStruct((ready.shape[0], 1), f32),
        ],
        [VMEM] * 2,
        0,
    )(ready, weight)
    third = total // 2
    *sent, txt_own, col_ids = call(
        functools.partial(unit_body, order, n_img),
        [shape(third, texts)] * 2 + [shape(total, texts), jax.ShapeDtypeStruct((1, 2 * total), jnp.int32)],
        [SMEM, ANY] + [VMEM] * len(txt_parts),
        0,
    )(place, ready_hidden[2], *txt_parts)
    txt_sib = join(*[core(part) for part in sent])
    early = [ready, near]
    last = link(near, True)

    def batch(images, order, cost, before):
        held = len(order) * rows
        first = held > images.shape[0]
        term = jax.ShapeDtypeStruct((rows, features), f32)
        return call(
            functools.partial(batch_body, first, order, n_txt),
            [shape(held, texts), term, term],
            [SMEM] + [VMEM] * (7 + len(before)),
            cost,
            [
                pltpu.VMEM((held, features), f32),
                pltpu.VMEM((held, features), bf16),
                pltpu.VMEM((held, 2 * total), bf16),
            ],
        )(place, scale, bias, images, weight, txt_own, txt_sib, col_ids, *before)

    d_early, own, sib = batch(near, early_order, 1_400_000_000, ready_hidden)
    d_early_sib = core(d_early)
    early_sib = [core(after(ready, d_early)), core(near)]
    head = jax.ShapeDtypeStruct((emb, features), f32)

    def head_terms(images, d_hidden, *before):
        refs = [*images, *d_hidden, *before]
        body = functools.partial(head_body, len(images), len(d_hidden))
        return call(body, head, [VMEM] * len(refs), 0)(*refs)

    before = head_terms(early, [d_early])
    img_last = [join(after(far, before, early_sib[1]), last)]
    late_sib = [core(part) for part in img_last]
    d_late, own, sib = batch(img_last[0], late_order, 6_000_000_000, [own, sib])
    d_late_sib = core(d_late)
    received = core(sib)

    before = head_terms(early_sib, [d_early_sib], before)
    left = img_last + late_sib
    right = [d_late, d_late_sib]
    sizes = [256, 384, emb - 640] if emb % 128 == 0 and emb > 640 else [emb]
    head_grad, text_grads, image_grads = pl.pallas_call(
        functools.partial(last_body, len(left), len(right), sizes),
        out_shape=[head, shape(rows, texts), shape(rows, images)],
        in_specs=[VMEM] * (len(left) + len(right) + 7),
        out_specs=[ANY] * 3,
        scratch_shapes=[
            pltpu.VMEM(head.shape, f32),
            pltpu.VMEM(texts.shape, bf16),
            pltpu.VMEM(images.shape, bf16),
            pltpu.SemaphoreType.DMA((len(sizes) + 2,)),
        ],
        compiler_params=pltpu.CompilerParams(vmem_limit_bytes=LIMIT),
        cost_estimate=pl.CostEstimate(flops=0, bytes_accessed=0, transcendentals=0),
    )(scale, txt_own_block, own, received, weight, d_early, *left, *right, before)
    return image_grads, text_grads, head_grad


def blocked(images, texts, head_weight, log_scale, logit_bias):
    scale = jnp.exp(log_scale[0])
    bias = logit_bias[0]
    hidden = jnp.dot(images, head_weight, preferred_element_type=f32)
    img_inv = lax.rsqrt(jnp.sum(hidden * hidden, axis=1, keepdims=True) + eps)
    img_unit = (hidden * img_inv).astype(bf16)
    txt_full = texts.astype(f32)
    txt_inv = lax.rsqrt(jnp.sum(txt_full * txt_full, axis=1, keepdims=True) + eps)
    txt_unit = (txt_full * txt_inv).astype(bf16)
    img_block = lax.all_gather(img_unit, "txt", axis=0, tiled=True)
    txt_block = lax.all_gather(txt_unit, "img", axis=0, tiled=True)
    total_rows = img_block.shape[0]
    total_cols = txt_block.shape[0]
    features = img_block.shape[1]
    row_first = lax.axis_index("img") * total_rows
    col_first = lax.axis_index("txt") * total_cols
    columns = col_first + jnp.arange(total_cols, dtype=jnp.int32)
    width = 512 if total_rows % 512 == 0 else total_rows
    count = total_rows // width
    blocks = img_block.reshape(count, width, features)

    def step(carry, inputs):
        block, index = inputs
        logits = scale * dot(block, txt_block, NT) + bias
        row_ids = row_first + index * width + jnp.arange(width, dtype=jnp.int32)
        label = jnp.where(row_ids[:, None] == columns[None, :], 1.0, -1.0).astype(f32)
        grad = (-label * jax.nn.sigmoid(-label * logits)).astype(bf16)
        d_rows = scale * dot(grad, txt_block)
        carry = carry + scale * dot(grad, block, TN)
        return (carry, d_rows)

    txt_terms, row_terms = lax.scan(
        step,
        jnp.zeros((total_cols, features), f32),
        (blocks, jnp.arange(count, dtype=jnp.int32)),
    )
    img_terms = row_terms.reshape(total_rows, features)
    d_img = lax.psum_scatter(
        img_terms.astype(bf16), "txt", scatter_dimension=0, tiled=True
    ).astype(f32)
    inner = jnp.sum(hidden * d_img, axis=1, keepdims=True)
    d_hidden = (img_inv * (d_img - hidden * img_inv * img_inv * inner)).astype(bf16)
    image_grads = dot(d_hidden, head_weight, NT).astype(bf16)
    head_grad = lax.psum(dot(images, d_hidden, TN), ("img", "txt"))
    d_txt = lax.psum_scatter(
        txt_terms.astype(bf16), "img", scatter_dimension=0, tiled=True
    ).astype(f32)
    inner_txt = jnp.sum(txt_full * d_txt, axis=1, keepdims=True)
    text_grads = (txt_inv * (d_txt - txt_full * txt_inv * txt_inv * inner_txt)).astype(bf16)
    return (image_grads, text_grads, head_grad)


def solution(mesh):
    n_img, n_txt = mesh.shape["img"], mesh.shape["txt"]

    def shards(images, texts, head_weight, log_scale, logit_bias):
        width = images.shape[1] + texts.shape[1]
        held = 2 * n_img * n_txt * images.shape[0] * width
        same = images.shape[0] == texts.shape[0]
        if (n_img, n_txt) == (4, 8) and same and held <= GATHER_BYTES:
            return gathered(n_img, n_txt, images, texts, head_weight, log_scale, logit_bias)
        return blocked(images, texts, head_weight, log_scale, logit_bias)

    return jax.shard_map(
        shards,
        mesh=mesh,
        in_specs=(P(("img", "txt"), None), P(("txt", "img"), None), P(), P(), P()),
        out_specs=(P(("img", "txt"), None), P(("txt", "img"), None), P()),
        check_vma=False,
    )
```
